256 devices in a mesh: col: 32 (over z, x), row: 8 (over y, core).
Axes of the slice: x: 4, y: 4, z: 8, core: 2. Of those that a mesh axis runs over, the one named last changes fastest.
Arguments:
- panel: bfloat16 [4096, 4096], P('row', 'col'), may hold values from -0.09375 to 0.09375
- inv_factor: bfloat16 [4096, 4096], P('col'), as said below
- fill: int32 [32, 32], replicated, may hold values from 0 to 1, as said below
- owner: int32 [32], replicated, may hold values from 0 to 31, as said below
- trailing: float32 [4096, 4096], P('row', 'col'), may hold values from -6 to 6
- cotangent: float32 [4096, 4096], P('row', 'col'), may hold values from -6 to 6
Outputs:
- updated: float32 [4096, 4096], P('row', 'col')
- panel_grad: float32 [4096, 4096], P('row', 'col')
The draws below stay inside these ranges and needn't reach their ends.
Inputs may be any that keep to these rules, and one draw needn't show every extreme that they name: fill is 1 on the diagonal, 0 above it, and 0 or 1 below it. `owner`: every col index owns exactly 1 block column. inv_factor is upper triangular with a positive diagonal.
All inputs are finite; a program needn't handle non-finite values.
Results may differ from the reference program's by a relative error of at most 0.0047.
Values may be sent and summed in bfloat16 or wider, within the bound.
No kernel may reach another device: no remote copies, remote signals or barrier semaphores. Data moves between devices by JAX's collectives and lax.ppermute only.
A program may use at most 128 MiB of HBM per device.

```python
import math
import jax
import jax.numpy as jnp

W = 4096
BS = 128
BCOL = 1
NB = 32
PR = 4096


def draw_inv_factor(key, part):
    key = jax.random.fold_in(key, 11)
    key_off, key_diag = jax.random.split(key)
    rows_at = jnp.arange(W)[:, None]
    cols_at = jnp.arange(W)[None, :]
    spread = jax.random.normal(key_off, (W, W), jnp.float32) * (0.6 / math.sqrt(W))
    diagonal = jax.random.uniform(key_diag, (W,), jnp.float32, 0.6, 1.4)
    upper = jnp.where(cols_at > rows_at, spread, 0.0)
    result = upper + jnp.where(cols_at == rows_at, diagonal[None, :], 0.0)
    return result.astype(jnp.bfloat16)


def draw_fill(key, part):
    key = jax.random.fold_in(key, 23)
    coins = jax.random.randint(key, (NB, NB), 0, 2, dtype=jnp.int32)
    rows_at = jnp.arange(NB)[:, None]
    cols_at = jnp.arange(NB)[None, :]
    below = jnp.where(rows_at > cols_at, coins, 0)
    return (below + (rows_at == cols_at).astype(jnp.int32)).astype(jnp.int32)


def draw_owner(key, part):
    key = jax.random.fold_in(key, 37)
    order = jax.random.permutation(key, NB)
    return (order // BCOL).astype(jnp.int32)


def shard_levels(stream_key, extent, shards, least, top_value):
    level, own = 1.0, jax.random.fold_in(stream_key, 6)
    for axis_at, parts in shards:
        steps = jnp.exp(jax.random.uniform(jax.random.fold_in(own, axis_at), (parts,), jnp.float32, least / len(shards), top_value / len(shards)))
        level = level * jnp.repeat(steps, extent[axis_at] // parts).reshape([-1 if axis == axis_at else 1 for axis in range(len(extent))])
    return level


def bell_draw(own_key, extent, scale, bound, shards=(), held_as=jnp.bfloat16):
    level = shard_levels(own_key, extent, shards, -0.22, 0.18) if shards else 1.0
    values = jax.random.normal(own_key, extent, jnp.float32) * scale * level
    return jnp.minimum(jnp.maximum(values, -bound), bound).astype(held_as)


def setup_inputs(seed: int = 0) -> dict:
    keys = jax.random.split(jax.random.key(seed), 7)
    return {
        "panel": bell_draw(keys[0], (PR, W), W ** -0.5, 0.09375, ((0, 8), (1, 32))),
        "inv_factor": draw_inv_factor(jax.random.fold_in(keys[6], 71), 0),
        "fill": draw_fill(jax.random.fold_in(keys[6], 71), 0),
        "owner": draw_owner(jax.random.fold_in(keys[6], 71), 0),
        "trailing": bell_draw(keys[4], (PR, NB * BS), 1.0, 6.0, ((0, 8), (1, 32)), jnp.float32),
        "cotangent": bell_draw(keys[5], (PR, NB * BS), 1.0, 6.0, ((0, 8), (1, 32)), jnp.float32),
    }


def slot_table(owner):
    count = owner.shape[0]
    index = jnp.arange(count, dtype=jnp.int32)
    same = (owner[:, None] == owner[None, :]) & (index[None, :] < index[:, None])
    rank = jnp.sum(same.astype(jnp.int32), axis=1)
    slot = owner * BCOL + rank
    hits = (slot[None, :] == index[:, None]).astype(jnp.int32)
    column_of_slot = jnp.sum(hits * index[None, :], axis=1).astype(jnp.int32)
    return slot.astype(jnp.int32), column_of_slot


def reference(panel, inv_factor, fill, owner, trailing, cotangent):
    factor = jnp.dot(panel, inv_factor, preferred_element_type=jnp.float32).astype(jnp.bfloat16)
    slot, column_of_slot = slot_table(owner)
    blocks = factor.reshape(NB, BS, W)
    owned = blocks[column_of_slot].reshape(NB * BS, W)
    block_mask = fill[:, column_of_slot].astype(jnp.float32)
    mask = jnp.repeat(jnp.repeat(block_mask, BS, axis=0), BS, axis=1)
    products = jnp.dot(factor, owned.T, preferred_element_type=jnp.float32)
    updated = trailing - mask * products
    weighted = (mask * cotangent).astype(jnp.bfloat16)
    own_term = jnp.dot(weighted, owned, preferred_element_type=jnp.float32)
    column_term = jnp.dot(weighted.T, factor, preferred_element_type=jnp.float32)
    moved_term = column_term.reshape(NB, BS, W)[slot].reshape(PR, W)
    factor_grad = (-(own_term + moved_term)).astype(jnp.bfloat16)
    panel_grad = jnp.dot(factor_grad, inv_factor.T, preferred_element_type=jnp.float32)
    return updated, panel_grad
```

```python
import jax
import jax.numpy as jnp
from jax import lax
from jax.experimental import pallas as pl
from jax.experimental.pallas import tpu as pltpu
from jax.sharding import PartitionSpec as P

BS = 128
NZ = 8
NX = 4
NR = 8
NS = 32
ROWS = 512
BF = jnp.bfloat16
F32 = jnp.float32
X_GROUPS = [[z * NX + x for x in range(NX)] for z in range(NZ)]
Z_GROUPS = [[z * NX + x for z in range(NZ)] for x in range(NX)]
VMEM = pl.BlockSpec(memory_space=pltpu.VMEM)
SMEM = pl.BlockSpec(memory_space=pltpu.SMEM)


def call(kernel, out_shape, in_specs, flops, nbytes):
    many = isinstance(out_shape, (tuple, list))
    return pl.pallas_call(
        kernel,
        out_shape=out_shape,
        in_specs=in_specs,
        out_specs=[VMEM] * len(out_shape) if many else VMEM,
        compiler_params=pltpu.CompilerParams(vmem_limit_bytes=40 * 1024 * 1024),
        cost_estimate=pl.CostEstimate(flops=flops, bytes_accessed=nbytes, transcendentals=0),
    )


def exchange_x(value):
    return lax.all_to_all(value, "col", 0, 0, axis_index_groups=X_GROUPS)


def exchange_z(value):
    return lax.all_to_all(value, "col", 0, 0, axis_index_groups=Z_GROUPS)


def exchange_row(value):
    return lax.all_to_all(value, "row", 0, 0)


def factor_kernel(got_ref, out_ref):
    left = jnp.concatenate([got_ref[x, :ROWS, :] for x in range(NX)], axis=1)
    for z in range(0, NZ, 2):
        right = jnp.concatenate(
            [
                jnp.concatenate(
                    [got_ref[x, ROWS + (z + h) * BS : ROWS + (z + h + 1) * BS, :] for h in range(2)],
                    axis=1,
                )
                for x in range(NX)
            ],
            axis=0,
        )
        product = jnp.dot(left, right, preferred_element_type=F32).astype(BF)
        out_ref[z] = product[:, :BS]
        out_ref[z + 1] = product[:, BS:]


def pair_kernel(factor_ref, got_ref, owned_ref, out_ref):
    left = jnp.concatenate([factor_ref[z] for z in range(NZ)], axis=1)
    for x in range(NX):
        right = jnp.concatenate(
            [
                jnp.concatenate(
                    [got_ref[x, ROWS + z * BS : ROWS + (z + 1) * BS, :] for z in range(NZ)], axis=1
                ),
                jnp.concatenate([owned_ref[z, x] for z in range(NZ)], axis=1),
            ],
            axis=0,
        )
        product = lax.dot_general(
            left, right, (((1,), (1,)), ((), ())), preferred_element_type=F32
        ).astype(BF)
        out_ref[x, 0] = product[:, :BS]
        out_ref[x, 1] = product[:, BS:]


def column_kernel(perm_ref, weighted_ref, piece_ref, out_ref):
    piece = piece_ref[...]
    for s in range(0, NS, 2):
        left = jnp.concatenate([weighted_ref[s], weighted_ref[s + 1]], axis=1)
        product = lax.dot_general(
            left, piece, (((0,), (0,)), ((), ())), preferred_element_type=F32
        ).astype(BF)
        out_ref[perm_ref[s]] = product[:BS]
        out_ref[perm_ref[s + 1]] = product[BS:]


def own_kernel(perm_ref, weighted_ref, got_ref, out_ref):
    step = 4
    total = jnp.zeros((ROWS, BS), F32)
    for s in range(0, NS, step):
        left = jnp.concatenate([weighted_ref[s + h] for h in range(step)], axis=1)
        right = []
        for h in range(step):
            j = perm_ref[s + h]
            right.append(got_ref[j // 4, pl.ds(pl.multiple_of((j % 4) * BS, BS), BS), :])
        total += jnp.dot(left, jnp.concatenate(right, axis=0), preferred_element_type=F32)
    for r in range(NR):
        total += got_ref[r, ROWS:, :].astype(F32)
    out_ref[...] = -total


def on_device(panel, inv_factor, fill, owner, trailing, cotangent):
    col = lax.axis_index("col")
    row = lax.axis_index("row")
    index = jnp.arange(NS, dtype=jnp.int32)
    perm = jnp.sum(jnp.where(owner[None, :] == index[:, None], index[None, :], 0), axis=1)
    mine = lax.dynamic_slice_in_dim(perm, col, 1)
    fill_rows = lax.dynamic_slice_in_dim(fill, row * 4, 4, 0)
    block_mask = jnp.sum(jnp.where(index[None, :] == mine[None, :], fill_rows, 0), axis=1)
    mask = block_mask.astype(F32)[:, None, None]

    weighted = (mask * cotangent.reshape(4, BS, BS)).astype(BF).reshape(ROWS, BS)
    weighted_all = lax.all_gather(weighted, "col", axis=0)

    columns = inv_factor.reshape(BS, NZ, NX, BS).transpose(2, 1, 0, 3).reshape(NX, NZ * BS, BS)
    sent = jnp.concatenate([jnp.broadcast_to(panel[None], (NX, ROWS, BS)), columns], axis=1)
    got = exchange_x(sent)
    partial = call(
        factor_kernel, jax.ShapeDtypeStruct((NZ, ROWS, BS), BF), [VMEM], 2 * 512 * 512 * 1024, 3 << 20
    )(got)
    factor = jnp.sum(exchange_z(partial).astype(F32), axis=0).astype(BF)

    factor_k = exchange_z(jnp.broadcast_to(factor[None], (NZ, ROWS, BS)))
    factor_col = exchange_row(jnp.broadcast_to(factor[None], (NR, ROWS, BS)))
    picked = factor_col.reshape(NS, BS, BS)[perm].reshape(NZ, NX, BS, BS)
    owned = exchange_z(picked)
    pair = call(
        pair_kernel,
        jax.ShapeDtypeStruct((NX, 2, ROWS, BS), BF),
        [VMEM] * 3,
        2 * 512 * 1024 * 1024,
        5 << 20,
    )(factor_k, got, owned)
    pair_sum = jnp.sum(exchange_x(pair).astype(F32), axis=0)
    piece = pair_sum[0].astype(BF)
    updated = (
        trailing.reshape(4, BS, BS) - mask * pair_sum[1].reshape(4, BS, BS)
    ).reshape(ROWS, BS)

    column = call(
        column_kernel,
        jax.ShapeDtypeStruct((NS, BS, BS), BF),
        [SMEM, VMEM, VMEM],
        2 * 512 * 4096 * 128,
        6 << 20,
    )(perm, weighted_all, piece)
    last = exchange_row(
        jnp.concatenate(
            [jnp.broadcast_to(piece[None], (NR, ROWS, BS)), column.reshape(NR, ROWS, BS)], axis=1
        )
    )
    panel_grad = call(
        own_kernel,
        jax.ShapeDtypeStruct((ROWS, BS), F32),
        [SMEM, VMEM, VMEM],
        2 * 512 * 4096 * 128,
        7 << 20,
    )(perm, weighted_all, last)
    return updated, panel_grad


def solution(mesh):
    return jax.shard_map(
        on_device,
        mesh=mesh,
        in_specs=(P("row", "col"), P("col", None), P(), P(), P("row", "col"), P("row", "col")),
        out_specs=(P("row", "col"), P("row", "col")),
        check_vma=False,
    )
```

```python
import jax
import jax.numpy as jnp
from jax import lax
from jax.experimental import pallas as pl
from jax.experimental.pallas import tpu as pltpu
from jax.sharding import PartitionSpec as P

BS = 128
NZ = 8
NX = 4
NR = 8
NS = 32
ROWS = 512
BF = jnp.bfloat16
F32 = jnp.float32
X_GROUPS = [[z * NX + x for x in range(NX)] for z in range(NZ)]
Z_GROUPS = [[z * NX + x for z in range(NZ)] for x in range(NX)]
VMEM = pl.BlockSpec(memory_space=pltpu.VMEM)
SMEM = pl.BlockSpec(memory_space=pltpu.SMEM)


def call(kernel, out_shape, in_specs, flops, nbytes):
    many = isinstance(out_shape, (tuple, list))
    return pl.pallas_call(
        kernel,
        out_shape=out_shape,
        in_specs=in_specs,
        out_specs=[VMEM] * len(out_shape) if many else VMEM,
        compiler_params=pltpu.CompilerParams(vmem_limit_bytes=40 * 1024 * 1024),
        cost_estimate=pl.CostEstimate(flops=flops, bytes_accessed=nbytes, transcendentals=0),
    )


def exchange_x(value):
    return lax.all_to_all(value, "col", 0, 0, axis_index_groups=X_GROUPS)


def exchange_z(value):
    return lax.all_to_all(value, "col", 0, 0, axis_index_groups=Z_GROUPS)


def exchange_row(value):
    return lax.all_to_all(value, "row", 0, 0)


def factor_kernel(got_ref, out_ref):
    left = jnp.concatenate([got_ref[x, :ROWS, :] for x in range(NX)], axis=1)
    for z in range(0, NZ, 2):
        right = jnp.concatenate(
            [
                jnp.concatenate(
                    [got_ref[x, ROWS + (z + h) * BS : ROWS + (z + h + 1) * BS, :] for h in range(2)],
                    axis=1,
                )
                for x in range(NX)
            ],
            axis=0,
        )
        product = jnp.dot(left, right, preferred_element_type=F32).astype(BF)
        out_ref[z] = product[:, :BS]
        out_ref[z + 1] = product[:, BS:]


def pair_kernel(factor_ref, got_ref, owned_ref, out_ref):
    left = jnp.concatenate([factor_ref[z] for z in range(NZ)], axis=1)
    for x in range(NX):
        right = jnp.concatenate(
            [
                jnp.concatenate(
                    [got_ref[x, ROWS + z * BS : ROWS + (z + 1) * BS, :] for z in range(NZ)], axis=1
                ),
                jnp.concatenate([owned_ref[z, x] for z in range(NZ)], axis=1),
            ],
            axis=0,
        )
        product = lax.dot_general(
            left, right, (((1,), (1,)), ((), ())), preferred_element_type=F32
        ).astype(BF)
        out_ref[x, 0] = product[:, :BS]
        out_ref[x, 1] = product[:, BS:]


def column_kernel(perm_ref, weighted_ref, piece_ref, out_ref):
    piece = piece_ref[...]
    for s in range(0, NS, 2):
        left = jnp.concatenate([weighted_ref[s], weighted_ref[s + 1]], axis=1)
        product = lax.dot_general(
            left, piece, (((0,), (0,)), ((), ())), preferred_element_type=F32
        ).astype(BF)
        out_ref[perm_ref[s]] = product[:BS]
        out_ref[perm_ref[s + 1]] = product[BS:]


def own_kernel(perm_ref, weighted_ref, got_ref, out_ref):
    step = 4
    total = jnp.zeros((ROWS, BS), F32)
    for s in range(0, NS, step):
        left = jnp.concatenate([weighted_ref[s + h] for h in range(step)], axis=1)
        right = []
        for h in range(step):
            j = perm_ref[s + h]
            right.append(got_ref[j // 4, pl.ds(pl.multiple_of((j % 4) * BS, BS), BS), :])
        total += jnp.dot(left, jnp.concatenate(right, axis=0), preferred_element_type=F32)
    for r in range(NR):
        total += got_ref[r, ROWS:, :].astype(F32)
    out_ref[...] = -total


def on_device(panel, inv_factor, fill, owner, trailing, cotangent):
    col = lax.axis_index("col")
    row = lax.axis_index("row")
    index = jnp.arange(NS, dtype=jnp.int32)
    perm = jnp.sum(jnp.where(owner[None, :] == index[:, None], index[None, :], 0), axis=1)
    mine = lax.dynamic_slice_in_dim(perm, col, 1)
    fill_rows = lax.dynamic_slice_in_dim(fill, row * 4, 4, 0)
    block_mask = jnp.sum(jnp.where(index[None, :] == mine[None, :], fill_rows, 0), axis=1)
    mask = block_mask.astype(F32)[:, None, None]

    weighted = (mask * cotangent.reshape(4, BS, BS)).astype(BF).reshape(ROWS, BS)

    columns = inv_factor.reshape(BS, NZ, NX, BS).transpose(2, 1, 0, 3).reshape(NX, NZ * BS, BS)
    sent = jnp.concatenate([jnp.broadcast_to(panel[None], (NX, ROWS, BS)), columns], axis=1)
    sent, weighted = lax.optimization_barrier((sent, weighted))
    got = exchange_x(sent)
    weighted_all = lax.all_gather(weighted, "col", axis=0)
    partial = call(
        factor_kernel, jax.ShapeDtypeStruct((NZ, ROWS, BS), BF), [VMEM], 2 * 512 * 512 * 1024, 3 << 20
    )(got)
    factor = jnp.sum(exchange_z(partial).astype(F32), axis=0).astype(BF)

    factor_k = exchange_z(jnp.broadcast_to(factor[None], (NZ, ROWS, BS)))
    factor_col = exchange_row(jnp.broadcast_to(factor[None], (NR, ROWS, BS)))
    picked = factor_col.reshape(NS, BS, BS)[perm].reshape(NZ, NX, BS, BS)
    owned = exchange_z(picked)
    pair = call(
        pair_kernel,
        jax.ShapeDtypeStruct((NX, 2, ROWS, BS), BF),
        [VMEM] * 3,
        2 * 512 * 1024 * 1024,
        5 << 20,
    )(factor_k, got, owned)
    pair_sum = jnp.sum(exchange_x(pair).astype(F32), axis=0)
    piece = pair_sum[0].astype(BF)
    updated = (
        trailing.reshape(4, BS, BS) - mask * pair_sum[1].reshape(4, BS, BS)
    ).reshape(ROWS, BS)

    column = call(
        column_kernel,
        jax.ShapeDtypeStruct((NS, BS, BS), BF),
        [SMEM, VMEM, VMEM],
        2 * 512 * 4096 * 128,
        6 << 20,
    )(perm, weighted_all, piece)
    last = exchange_row(
        jnp.concatenate(
            [jnp.broadcast_to(piece[None], (NR, ROWS, BS)), column.reshape(NR, ROWS, BS)], axis=1
        )
    )
    panel_grad = call(
        own_kernel,
        jax.ShapeDtypeStruct((ROWS, BS), F32),
        [SMEM, VMEM, VMEM],
        2 * 512 * 4096 * 128,
        7 << 20,
    )(perm, weighted_all, last)
    return updated, panel_grad


def solution(mesh):
    return jax.shard_map(
        on_device,
        mesh=mesh,
        in_specs=(P("row", "col"), P("col", None), P(), P(), P("row", "col"), P("row", "col")),
        out_specs=(P("row", "col"), P("row", "col")),
        check_vma=False,
    )
```

```python
import jax
import jax.numpy as jnp
from jax import lax
from jax.experimental import pallas as pl
from jax.experimental.pallas import tpu as pltpu
from jax.sharding import PartitionSpec as P

BS = 128
NZ = 8
NX = 4
NY = 4
NS = 32
ROWS = 512
BF = jnp.bfloat16
F32 = jnp.float32
X_GROUPS = [[z * NX + x for x in range(NX)] for z in range(NZ)]
Z_GROUPS = [[z * NX + x for z in range(NZ)] for x in range(NX)]
VMEM = pl.BlockSpec(memory_space=pltpu.VMEM)
SMEM = pl.BlockSpec(memory_space=pltpu.SMEM)
TILE = jax.ShapeDtypeStruct((ROWS, BS), BF)
STACK = jax.ShapeDtypeStruct((NY, ROWS, BS), BF)


def call(kernel, out_shape, in_specs, flops, nbytes, vmem=24):
    many = isinstance(out_shape, (tuple, list))
    return pl.pallas_call(
        kernel,
        out_shape=out_shape,
        in_specs=in_specs,
        out_specs=[VMEM] * len(out_shape) if many else VMEM,
        compiler_params=pltpu.CompilerParams(vmem_limit_bytes=vmem * 1024 * 1024),
        cost_estimate=pl.CostEstimate(flops=flops, bytes_accessed=nbytes, transcendentals=0),
    )


def exchange_x(value):
    return lax.all_to_all(value, "col", 0, 0, axis_index_groups=X_GROUPS)


def exchange_z(value):
    return lax.all_to_all(value, "col", 0, 0, axis_index_groups=Z_GROUPS)


def shift_z(value, k):
    pairs = [(z * NX + x, (z + k) % NZ * NX + x) for z in range(NZ) for x in range(NX)]
    return lax.ppermute(value, "col", pairs)


def shift_x(value, k):
    pairs = [(z * NX + x, z * NX + (x + k) % NX) for z in range(NZ) for x in range(NX)]
    return lax.ppermute(value, "col", pairs)


def shift_y(value, k):
    pairs = [(y * 2 + c, (y + k) % NY * 2 + c) for y in range(NY) for c in range(2)]
    return lax.ppermute(value, "row", pairs)


def swap_core(value):
    return lax.ppermute(value, "row", [(r, r ^ 1) for r in range(2 * NY)])


def gather_y(value):
    return [value] + [shift_y(value, -k) for k in range(1, NY)]


def ring_z(value):
    up, down = [value], [value]
    half = value.shape[0] // 2
    for _ in range(3):
        up.append(shift_z(up[-1], 1))
        down.append(shift_z(down[-1], -1))
    last = jnp.concatenate([shift_z(up[-1][:half], 1), shift_z(down[-1][half:], -1)])
    return jnp.stack([value] + down[1:] + [last] + up[1:][::-1])


def factor_kernel(got_ref, out_ref):
    left = jnp.concatenate([got_ref[x, :ROWS, :] for x in range(NX)], axis=1)
    for z in range(0, NZ, 2):
        right = jnp.concatenate(
            [
                jnp.concatenate(
                    [got_ref[x, ROWS + (z + h) * BS : ROWS + (z + h + 1) * BS, :] for h in range(2)],
                    axis=1,
                )
                for x in range(NX)
            ],
            axis=0,
        )
        product = jnp.dot(left, right, preferred_element_type=F32).astype(BF)
        out_ref[z] = product[:, :BS]
        out_ref[z + 1] = product[:, BS:]


def sent_kernel(panel_ref, *refs):
    sent_ref = refs[-1]
    sent_ref[0, :ROWS, :] = panel_ref[...]
    for z in range(NZ):
        sent_ref[0, ROWS + z * BS : ROWS + (z + 1) * BS, :] = refs[z][...]


def weighted_kernel(at_ref, owner_ref, fill_ref, cotangent_ref, weighted_ref, perm_ref):
    for j in range(NS):
        perm_ref[owner_ref[j]] = j
    mine = perm_ref[at_ref[3]]
    for i in range(4):
        scale = fill_ref[at_ref[4] * 4 + i, mine].astype(F32)
        rows = slice(i * BS, (i + 1) * BS)
        weighted_ref[:, rows] = (scale * cotangent_ref[rows, :]).T.astype(BF)


def tail_kernel(at_ref, perm_ref, fill_ref, trailing_ref, got_ref, out_ref):
    mine = perm_ref[at_ref[3]]
    for i in range(4):
        scale = fill_ref[at_ref[4] * 4 + i, mine].astype(F32)
        rows = slice(i * BS, (i + 1) * BS)
        total = got_ref[0, rows, :].astype(F32)
        for x in range(1, NX):
            total += got_ref[x, rows, :].astype(F32)
        out_ref[rows, :] = trailing_ref[rows, :] - scale * total


def inner_kernel(at_ref, got_ref, factor_ref, *outs):
    right = jnp.concatenate([factor_ref[z] for z in range(NZ)], axis=1)
    for k in range(NX):
        x = lax.rem(at_ref[5] + k, NX)
        blocks = [got_ref[x, ROWS + z * BS : ROWS + (z + 1) * BS, :] for z in range(NZ)]
        left = jnp.concatenate(blocks, axis=1)
        product = lax.dot_general(
            left, right, (((1,), (1,)), ((), ())), preferred_element_type=F32
        )
        for i in range(4):
            outs[k][i] = product[:, i * BS : (i + 1) * BS].astype(outs[k].dtype)


def outer_kernel(at_ref, same_ref, other_ref, factor_ref, out_ref):
    left = jnp.concatenate([factor_ref[z] for z in range(NZ)], axis=1)
    for k, owned_ref in enumerate((same_ref, other_ref)):
        rows = []
        for h in range(2):
            blocks = [owned_ref[z, h] for z in range(NZ)]
            rows.append(jnp.concatenate(blocks, axis=1))
        right = jnp.concatenate(rows, axis=0)
        product = lax.dot_general(
            left, right, (((1,), (1,)), ((), ())), preferred_element_type=F32
        ).astype(BF)
        x = 2 * lax.rem(at_ref[2] + k, 2)
        out_ref[x] = product[:, :BS]
        out_ref[x + 1] = product[:, BS:]


def place(at_ref, j):
    y = lax.rem(j // 8 + NY - at_ref[1], NY)
    c = lax.rem(j // 4 + at_ref[2], 2)
    return c, y, j % 4


def pick_kernel(at_ref, perm_ref, both_ref, out_ref):
    for s in range(NS // 2):
        c, y, i = place(at_ref, perm_ref[s // 2 * NX + s % 2 + 2 * at_ref[2]])
        out_ref[s] = both_ref[c, y, i]


def quarters(at_ref, perm_ref, refs):
    own, one, two_a, two_b, three = refs
    for k, pair in enumerate(((own, own), (one, one), (two_a, two_b), (three, three))):
        for h in range(2):
            ref = pair[h]
            first = h * 4 if ref.shape[0] == NZ else 0
            places = []
            for d in range(4 * h, 4 * h + 4):
                z = lax.rem(at_ref[0] + d, NZ)
                x = lax.rem(at_ref[5] + k, NX)
                places.append(place(at_ref, perm_ref[z * NX + x]))
            yield places, ref[first : first + 4].reshape(4 * BS, ROWS)


def column_kernel(at_ref, perm_ref, *refs):
    piece_ref, out_ref = refs[5:]
    piece = jnp.concatenate([piece_ref[i] for i in range(4)], axis=1)
    for places, left in quarters(at_ref, perm_ref, refs[:5]):
        product = lax.dot_general(
            left, piece, (((1,), (1,)), ((), ())), preferred_element_type=F32
        ).astype(BF)
        for h, (c, y, i) in enumerate(places):
            out_ref[c, y, i] = product[h * BS : (h + 1) * BS]


def own_kernel(at_ref, perm_ref, *refs):
    both_ref, out_ref = refs[5:]
    total = jnp.zeros((BS, ROWS), F32)
    for places, right in quarters(at_ref, perm_ref, refs[:5]):
        left = jnp.concatenate([both_ref[c, y, i] for c, y, i in places], axis=1)
        total += jnp.dot(left, right, preferred_element_type=F32)
    out_ref[...] = total.T


def both_cores(pieces):
    same = jnp.stack(pieces).reshape(NY, 4, BS, BS)
    return jnp.stack([same, swap_core(same)])


def whole(shape):
    return pl.BlockSpec(shape, lambda g: (0,) * len(shape))


def sweep(kernel, out_shape, out_type, *args):
    return call(
        kernel,
        jax.ShapeDtypeStruct(out_shape, out_type),
        [SMEM] * 2 + [VMEM] * 6,
        2 * 512 * 4096 * 128,
        6 << 20,
        16,
    )(*args)


def on_device(panel, inv_factor, fill, owner, trailing, cotangent):
    col = lax.axis_index("col")
    row = lax.axis_index("row")
    at = jnp.stack([col // NX, row // 2, row % 2, col, row, col % NX]).astype(jnp.int32)
    sent = pl.pallas_call(
        sent_kernel,
        grid=(NX,),
        out_shape=jax.ShapeDtypeStruct((NX, ROWS + NZ * BS, BS), BF),
        in_specs=[whole((ROWS, BS))]
        + [pl.BlockSpec((BS, BS), lambda g, z=z: (0, z * NX + g)) for z in range(NZ)],
        out_specs=pl.BlockSpec((1, ROWS + NZ * BS, BS), lambda g: (g, 0, 0)),
        cost_estimate=pl.CostEstimate(flops=0, bytes_accessed=3 << 20, transcendentals=0),
    )(panel, *([inv_factor] * NZ))
    weighted, perm = pl.pallas_call(
        weighted_kernel,
        out_shape=[
            jax.ShapeDtypeStruct((BS, ROWS), BF),
            jax.ShapeDtypeStruct((NS,), jnp.int32),
        ],
        in_specs=[SMEM] * 3 + [VMEM],
        out_specs=[VMEM, SMEM],
        compiler_params=pltpu.CompilerParams(vmem_limit_bytes=16 * 1024 * 1024),
        cost_estimate=pl.CostEstimate(flops=0, bytes_accessed=1 << 19, transcendentals=0),
    )(at, owner, fill, cotangent)
    got, near = lax.optimization_barrier((exchange_x(sent), ring_z(weighted)))

    partial = call(
        factor_kernel, jax.ShapeDtypeStruct((NZ, ROWS, BS), BF), [VMEM], 2 * 512 * 512 * 1024, 3 << 20
    )(got)
    parts, one, three = lax.optimization_barrier(
        (exchange_z(partial), shift_x(near, -1), shift_x(near, 1))
    )
    factor = jnp.sum(parts.astype(F32), axis=0).astype(BF)
    two_a, two_b = shift_x(three[:4], 1), shift_x(one[4:], -1)

    factor_k = exchange_z(jnp.broadcast_to(factor[None], (NZ, ROWS, BS)))
    picked = call(
        pick_kernel, jax.ShapeDtypeStruct((NS // 2, BS, BS), BF), [SMEM] * 2 + [VMEM], 0, 2 << 20
    )(at, perm, both_cores(gather_y(factor))).reshape(NZ, 2, BS, BS)
    owned = exchange_z(picked)
    inner = call(
        inner_kernel,
        [jax.ShapeDtypeStruct((4, BS, BS), F32)] + [jax.ShapeDtypeStruct((4, BS, BS), BF)] * 3,
        [SMEM] + [VMEM] * 2,
        2 * 512 * 1024 * 512,
        4 << 20,
    )(at, got, factor_k)
    piece = inner[0]
    for k in range(1, NX):
        piece = piece + shift_x(inner[k], k).astype(F32)
    piece = piece.astype(BF)

    weights = (near, one, two_a, two_b, three)
    column = sweep(column_kernel, (2, NY, 4, BS, BS), BF, at, perm, *weights, piece)
    column, piece = lax.optimization_barrier((column, piece))
    column = column.reshape(2, NY, ROWS, BS)
    total = column[0].astype(F32) + swap_core(column[1]).astype(F32)
    moved = total[0]
    for k in range(1, NY):
        moved = moved + shift_y(total[k].astype(BF), k).astype(F32)
    both = both_cores(gather_y(piece))
    own = sweep(own_kernel, (ROWS, BS), F32, at, perm, *weights, both)

    owned, _ = lax.optimization_barrier((owned, column))
    owned_other = swap_core(owned)
    outer = call(outer_kernel, STACK, [SMEM] + [VMEM] * 3, 2 * 512 * 1024 * 512, 4 << 20)(
        at, owned, owned_other, factor_k
    )
    updated = call(
        tail_kernel, jax.ShapeDtypeStruct((ROWS, BS), F32), [SMEM] * 3 + [VMEM] * 2, 0, 1 << 20
    )(at, perm, fill, trailing, exchange_x(outer))
    return updated, -(own + moved)


def solution(mesh):
    return jax.shard_map(
        on_device,
        mesh=mesh,
        in_specs=(P("row", "col"), P("col", None), P(), P(), P("row", "col"), P("row", "col")),
        out_specs=(P("row", "col"), P("row", "col")),
        check_vma=False,
    )
```

```python
import jax
import jax.numpy as jnp
from jax import lax
from jax.experimental import pallas as pl
from jax.experimental.pallas import tpu as pltpu
from jax.sharding import PartitionSpec as P

BS = 128
NZ = 8
NX = 4
NY = 4
NS = 32
ROWS = 512
BF = jnp.bfloat16
F32 = jnp.float32
X_GROUPS = [[z * NX + x for x in range(NX)] for z in range(NZ)]
Z_GROUPS = [[z * NX + x for z in range(NZ)] for x in range(NX)]
VMEM = pl.BlockSpec(memory_space=pltpu.VMEM)
SMEM = pl.BlockSpec(memory_space=pltpu.SMEM)
ANY = pl.BlockSpec(memory_space=pl.ANY)
TILE = jax.ShapeDtypeStruct((ROWS, BS), BF)
STACK = jax.ShapeDtypeStruct((NY, ROWS, BS), BF)


def call(kernel, out_shape, in_specs, flops, nbytes, vmem=12, out_specs=None, scratch=()):
    many = isinstance(out_shape, (tuple, list))
    if out_specs is None:
        out_specs = [VMEM] * len(out_shape) if many else VMEM
    return pl.pallas_call(
        kernel,
        out_shape=out_shape,
        in_specs=in_specs,
        out_specs=out_specs,
        scratch_shapes=list(scratch),
        compiler_params=pltpu.CompilerParams(vmem_limit_bytes=vmem * 1024 * 1024),
        cost_estimate=pl.CostEstimate(flops=flops, bytes_accessed=nbytes, transcendentals=0),
    )


def exchange_x(value):
    return lax.all_to_all(value, "col", 0, 0, axis_index_groups=X_GROUPS)


def exchange_z(value):
    return lax.all_to_all(value, "col", 0, 0, axis_index_groups=Z_GROUPS)


def shift_z(value, k):
    pairs = [(z * NX + x, (z + k) % NZ * NX + x) for z in range(NZ) for x in range(NX)]
    return lax.ppermute(value, "col", pairs)


def shift_x(value, k):
    pairs = [(z * NX + x, z * NX + (x + k) % NX) for z in range(NZ) for x in range(NX)]
    return lax.ppermute(value, "col", pairs)


def shift_y(value, k):
    pairs = [(y * 2 + c, (y + k) % NY * 2 + c) for y in range(NY) for c in range(2)]
    return lax.ppermute(value, "row", pairs)


def swap_core(value):
    return lax.ppermute(value, "row", [(r, r ^ 1) for r in range(2 * NY)])


def gather_y(value):
    return [value] + [shift_y(value, -k) for k in range(1, NY)]


def spread_kernel(total_ref, *refs):
    out_ref = refs[-1]
    for i in range(4):
        total = total_ref[i]
        for ref in refs[:3]:
            total += ref[i].astype(F32)
        total = total.astype(BF)
        refs[3][i] = total
        for r in range(2 * NY):
            out_ref[r, i] = total


def sum_kernel(parts_ref, tile_ref, out_ref):
    total = parts_ref[0].astype(F32)
    for z in range(1, NZ):
        total += parts_ref[z].astype(F32)
    total = total.astype(BF)
    tile_ref[...] = total
    for z in range(NZ):
        out_ref[z] = total


def factor_kernel(got_ref, out_ref):
    left = jnp.concatenate([got_ref[x, :ROWS, :] for x in range(NX)], axis=1)
    for z in range(0, NZ, 2):
        right = jnp.concatenate(
            [
                jnp.concatenate(
                    [got_ref[x, ROWS + (z + h) * BS : ROWS + (z + h + 1) * BS, :] for h in range(2)],
                    axis=1,
                )
                for x in range(NX)
            ],
            axis=0,
        )
        product = jnp.dot(left, right, preferred_element_type=F32).astype(BF)
        out_ref[z] = product[:, :BS]
        out_ref[z + 1] = product[:, BS:]


def sent_kernel(panel_ref, *refs):
    sent_ref = refs[-1]
    sent_ref[0, :ROWS, :] = panel_ref[...]
    for z in range(NZ):
        sent_ref[0, ROWS + z * BS : ROWS + (z + 1) * BS, :] = refs[z][...]


def weighted_kernel(at_ref, owner_ref, fill_ref, cotangent_ref, weighted_ref, meta_ref):
    for j in range(6):
        meta_ref[j] = at_ref[j]
    for j in range(NS):
        meta_ref[6 + owner_ref[j]] = j
    mine = meta_ref[6 + at_ref[3]]
    for i in range(4):
        scale = fill_ref[at_ref[4] * 4 + i, mine].astype(F32)
        rows = slice(i * BS, (i + 1) * BS)
        weighted_ref[:, rows] = (scale * cotangent_ref[rows, :]).T.astype(BF)


def tail_kernel(at_ref, fill_ref, trailing_ref, *refs):
    out_ref = refs[-1]
    mine = at_ref[6 + at_ref[3]]
    for i in range(4):
        scale = fill_ref[at_ref[4] * 4 + i, mine].astype(F32)
        rows = slice(i * BS, (i + 1) * BS)
        total = refs[0][rows, :]
        for ref in refs[1:4]:
            total += ref[rows, :].astype(F32)
        out_ref[rows, :] = trailing_ref[rows, :] - scale * total


def inner_kernel(at_ref, got_ref, factor_ref, *outs):
    right = jnp.concatenate([factor_ref[z] for z in range(NZ)], axis=1)
    rows = []
    for k in range(NX):
        x = lax.rem(at_ref[5] + k, NX)
        blocks = [got_ref[x, ROWS + z * BS : ROWS + (z + 1) * BS, :] for z in range(NZ)]
        rows.append(jnp.concatenate(blocks, axis=1))
    left = jnp.concatenate(rows, axis=0)
    product = lax.dot_general(left, right, (((1,), (1,)), ((), ())), preferred_element_type=F32)
    for k in range(NX):
        for i in range(4):
            block = product[k * BS : (k + 1) * BS, i * BS : (i + 1) * BS]
            outs[k][i] = block.astype(outs[k].dtype)


def outer_kernel(at_ref, same_ref, other_ref, factor_ref, *outs):
    left = jnp.concatenate([factor_ref[z] for z in range(NZ)], axis=1)
    rows = []
    for k in range(NX):
        x = lax.rem(at_ref[5] + k, NX)
        mine = x // 2 == at_ref[2]
        h = lax.rem(x, 2)
        blocks = [jnp.where(mine, same_ref[z, h], other_ref[z, h]) for z in range(NZ)]
        rows.append(jnp.concatenate(blocks, axis=1))
    right = jnp.concatenate(rows, axis=0)
    product = lax.dot_general(left, right, (((1,), (1,)), ((), ())), preferred_element_type=F32)
    for k in range(NX):
        outs[k][...] = product[:, k * BS : (k + 1) * BS].astype(outs[k].dtype)


def place(at_ref, j):
    y = lax.rem(j // 8 + NY - at_ref[1], NY)
    c = lax.rem(j // 4 + at_ref[2], 2)
    return c, y, j % 4


def chosen(at_ref, j, same_ref, other_ref):
    c, y, i = place(at_ref, j)
    return jnp.where(c == 0, same_ref[y, i], other_ref[y, i])


def pick_kernel(at_ref, same_ref, other_ref, out_ref):
    for s in range(NS // 2):
        j = at_ref[6 + s // 2 * NX + s % 2 + 2 * at_ref[2]]
        out_ref[s] = chosen(at_ref, j, same_ref, other_ref)


def quarters(at_ref, refs):
    own, one, two_a, two_b, three = refs
    for k, pair in enumerate(((own, own), (one, one), (two_a, two_b), (three, three))):
        for h in range(2):
            ref = pair[h]
            first = 4 * h if ref.shape[0] == NZ else 0
            slots = []
            for d in range(4 * h, 4 * h + 4):
                z = lax.rem(at_ref[0] + d, NZ)
                x = lax.rem(at_ref[5] + k, NX)
                slots.append(at_ref[6 + z * NX + x])
            yield slots, ref[first : first + 4].reshape(4 * BS, ROWS)


def column_kernel(at_ref, *refs):
    piece_ref, same_ref, other_ref, token_ref = refs[5:]
    piece = jnp.concatenate([piece_ref[i] for i in range(4)], axis=1)
    for slots, left in quarters(at_ref, refs[:5]):
        product = lax.dot_general(
            left, piece, (((1,), (1,)), ((), ())), preferred_element_type=F32
        ).astype(BF)
        for h, j in enumerate(slots):
            c, y, i = place(at_ref, j)
            part = product[h * BS : (h + 1) * BS]
            same_ref[jnp.where(c == 0, y, NY), i] = part
            other_ref[jnp.where(c == 0, NY, y), i] = part
    token_ref[...] = jnp.zeros(token_ref.shape, F32)


def total_kernel(same_ref, got_ref, keep_ref, *outs):
    keep_ref[...] = same_ref[0].astype(F32) + got_ref[0].astype(F32)
    for k in range(1, NY):
        outs[k - 1][...] = (same_ref[k].astype(F32) + got_ref[k].astype(F32)).astype(BF)


def own_kernel(at_ref, *refs):
    all_ref, out_ref = refs[5:]
    total = jnp.zeros((BS, ROWS), F32)
    for slots, right in quarters(at_ref, refs[:5]):
        left = jnp.concatenate([all_ref[j // 4, j % 4] for j in slots], axis=1)
        total += jnp.dot(left, right, preferred_element_type=F32)
    out_ref[...] = total.T


def final_kernel(own_ref, keep_ref, *refs):
    out_ref = refs[-1]
    for i in range(4):
        rows = slice(i * BS, (i + 1) * BS)
        total = own_ref[rows, :] + keep_ref[i]
        for ref in refs[:-1]:
            total += ref[i].astype(F32)
        out_ref[rows, :] = -total


def stack_kernel(*refs):
    out_ref = refs[-1]
    for k in range(NY):
        out_ref[k] = refs[k][...]


def both_cores(pieces, *after):
    pieces = [piece.reshape(4, BS, BS) for piece in pieces]
    same = call(
        stack_kernel,
        jax.ShapeDtypeStruct((NY, 4, BS, BS), BF),
        [VMEM] * NY + [ANY] * len(after),
        0,
        1 << 20,
    )(*pieces, *after)
    return same, swap_core(same)


def whole(shape):
    return pl.BlockSpec(shape, lambda g: (0,) * len(shape))


def sweep(kernel, out_shape, *args):
    return call(
        kernel, out_shape, [SMEM] + [VMEM] * (len(args) - 1), 2 * 512 * 4096 * 128, 6 << 20
    )(*args)


def on_device(panel, inv_factor, fill, owner, trailing, cotangent):
    col = lax.axis_index("col")
    row = lax.axis_index("row")
    at = jnp.stack([col // NX, row // 2, row % 2, col, row, col % NX]).astype(jnp.int32)
    sent = pl.pallas_call(
        sent_kernel,
        grid=(NX,),
        out_shape=jax.ShapeDtypeStruct((NX, ROWS + NZ * BS, BS), BF),
        in_specs=[whole((ROWS, BS))]
        + [pl.BlockSpec((BS, BS), lambda g, z=z: (0, z * NX + g)) for z in range(NZ)],
        out_specs=pl.BlockSpec((1, ROWS + NZ * BS, BS), lambda g: (g, 0, 0)),
        cost_estimate=pl.CostEstimate(flops=0, bytes_accessed=3 << 20, transcendentals=0),
    )(panel, *([inv_factor] * NZ))
    sent, cotangent = lax.optimization_barrier((sent, cotangent))
    weighted, at = pl.pallas_call(
        weighted_kernel,
        out_shape=[
            jax.ShapeDtypeStruct((BS, ROWS), BF),
            jax.ShapeDtypeStruct((NS + 6,), jnp.int32),
        ],
        in_specs=[SMEM] * 3 + [VMEM],
        out_specs=[VMEM, SMEM],
        compiler_params=pltpu.CompilerParams(vmem_limit_bytes=16 * 1024 * 1024),
        cost_estimate=pl.CostEstimate(flops=0, bytes_accessed=1 << 19, transcendentals=0),
    )(at, owner, fill, cotangent)
    u1, d1 = shift_z(weighted, 1), shift_z(weighted, -1)
    u2, d2 = shift_z(weighted, 2), shift_z(weighted, -2)
    u1, d1, u2, d2 = lax.optimization_barrier((u1, d1, u2, d2))
    u3, d3, d4 = shift_z(u2, 1), shift_z(d2, -1), shift_z(d2, -2)
    got, u1, u2, u3, d1, d2, d3, d4 = lax.optimization_barrier(
        (exchange_x(sent), u1, u2, u3, d1, d2, d3, d4)
    )
    near = jnp.stack([weighted, d1, d2, d3, d4, u3, u2, u1])

    tiles = jax.ShapeDtypeStruct((NZ, ROWS, BS), BF)
    partial = call(factor_kernel, tiles, [VMEM], 2 * 512 * 512 * 1024, 3 << 20)(got)
    parts, one, three = lax.optimization_barrier(
        (exchange_z(partial), shift_x(near, -1), shift_x(near, 1))
    )
    two_a, two_b = shift_x(three[:4], 1), shift_x(one[4:], -1)
    factor, spread = call(sum_kernel, [TILE, tiles], [VMEM], 0, 2 << 20)(parts)
    picked = call(
        pick_kernel, jax.ShapeDtypeStruct((NS // 2, BS, BS), BF), [SMEM] + [VMEM] * 2, 0, 2 << 20
    )(at, *both_cores(gather_y(factor), two_a, two_b))
    tile = jax.ShapeDtypeStruct((4, BS, BS), BF)
    total = jax.ShapeDtypeStruct((4, BS, BS), F32)
    token = jax.ShapeDtypeStruct((8, BS), F32)
    factor_k = exchange_z(spread)
    inner = call(
        inner_kernel,
        [total, tile, tile, tile],
        [SMEM] + [VMEM] * 2,
        2 * 512 * 1024 * 512,
        4 << 20,
    )(at, got, factor_k)
    owned = exchange_z(picked.reshape(NZ, 2, BS, BS))
    piece, spread = call(
        spread_kernel,
        [tile, jax.ShapeDtypeStruct((2 * NY, 4, BS, BS), BF)],
        [VMEM] * 4,
        0,
        2 << 20,
    )(inner[0], *[shift_x(inner[k], k) for k in range(1, NX)])

    weights = (near, one, two_a, two_b, three)
    blocks = jax.ShapeDtypeStruct((NY + 1, 4, BS, BS), BF)
    same, other, after = sweep(column_kernel, [blocks, blocks, token], at, *weights, piece)
    keep, *leave = call(total_kernel, [total] + [tile] * 3, [VMEM] * 2, 0, 2 << 20)(
        same, swap_core(other)
    )
    own = sweep(
        own_kernel,
        jax.ShapeDtypeStruct((ROWS, BS), F32),
        at,
        *weights,
        lax.all_to_all(spread, "row", 0, 0),
    )
    moved = [shift_y(value, k + 1) for k, value in enumerate(leave)]
    panel_grad = call(
        final_kernel, jax.ShapeDtypeStruct((ROWS, BS), F32), [VMEM] * 5, 0, 1 << 20
    )(own, keep, *moved)

    outer = call(
        outer_kernel,
        [jax.ShapeDtypeStruct((ROWS, BS), F32), TILE, TILE, TILE],
        [SMEM] + [VMEM] * 3,
        2 * 512 * 1024 * 512,
        4 << 20,
    )(at, owned, swap_core(owned), factor_k)
    updated = call(
        tail_kernel, jax.ShapeDtypeStruct((ROWS, BS), F32), [SMEM] * 2 + [VMEM] * 5, 0, 1 << 20
    )(at, fill, trailing, outer[0], *[shift_x(outer[k], k) for k in range(1, NX)])
    return updated, panel_grad


def solution(mesh):
    return jax.shard_map(
        on_device,
        mesh=mesh,
        in_specs=(P("row", "col"), P("col", None), P(), P(), P("row", "col"), P("row", "col")),
        out_specs=(P("row", "col"), P("row", "col")),
        check_vma=False,
    )
```

```python
import jax
import jax.numpy as jnp
from jax import lax
from jax.experimental import pallas as pl
from jax.experimental.pallas import tpu as pltpu
from jax.sharding import PartitionSpec as P

BS = 128
NZ = 8
NX = 4
NY = 4
NS = 32
ROWS = 512
BF = jnp.bfloat16
F32 = jnp.float32
X_GROUPS = [[z * NX + x for x in range(NX)] for z in range(NZ)]
Z_GROUPS = [[z * NX + x for z in range(NZ)] for x in range(NX)]
VMEM = pl.BlockSpec(memory_space=pltpu.VMEM)
SMEM = pl.BlockSpec(memory_space=pltpu.SMEM)
ANY = pl.BlockSpec(memory_space=pl.ANY)
TILE = jax.ShapeDtypeStruct((ROWS, BS), BF)
STACK = jax.ShapeDtypeStruct((NY, ROWS, BS), BF)


def call(kernel, out_shape, in_specs, flops, nbytes, vmem=12, out_specs=None, scratch=()):
    many = isinstance(out_shape, (tuple, list))
    if out_specs is None:
        out_specs = [VMEM] * len(out_shape) if many else VMEM
    return pl.pallas_call(
        kernel,
        out_shape=out_shape,
        in_specs=in_specs,
        out_specs=out_specs,
        scratch_shapes=list(scratch),
        compiler_params=pltpu.CompilerParams(vmem_limit_bytes=vmem * 1024 * 1024),
        cost_estimate=pl.CostEstimate(flops=flops, bytes_accessed=nbytes, transcendentals=0),
    )


def exchange_x(value):
    return lax.all_to_all(value, "col", 0, 0, axis_index_groups=X_GROUPS)


def exchange_z(value):
    return lax.all_to_all(value, "col", 0, 0, axis_index_groups=Z_GROUPS)


def shift_z(value, k):
    pairs = [(z * NX + x, (z + k) % NZ * NX + x) for z in range(NZ) for x in range(NX)]
    return lax.ppermute(value, "col", pairs)


def shift_x(value, k):
    pairs = [(z * NX + x, z * NX + (x + k) % NX) for z in range(NZ) for x in range(NX)]
    return lax.ppermute(value, "col", pairs)


def shift_y(value, k):
    pairs = [(y * 2 + c, (y + k) % NY * 2 + c) for y in range(NY) for c in range(2)]
    return lax.ppermute(value, "row", pairs)


def swap_core(value):
    return lax.ppermute(value, "row", [(r, r ^ 1) for r in range(2 * NY)])


def gather_y(value):
    return [value] + [shift_y(value, -k) for k in range(1, NY)]


def spread_kernel(total_ref, *refs):
    out_ref = refs[-1]
    for i in range(4):
        total = total_ref[i]
        for ref in refs[:3]:
            total += ref[i].astype(F32)
        total = total.astype(BF)
        refs[3][i] = total
        for r in range(2 * NY):
            out_ref[r, i] = total


def sum_kernel(parts_ref, tile_ref, out_ref):
    total = parts_ref[0].astype(F32)
    for z in range(1, NZ):
        total += parts_ref[z].astype(F32)
    total = total.astype(BF)
    tile_ref[...] = total
    for z in range(NZ):
        out_ref[z] = total


def factor_kernel(got_ref, out_ref):
    left = jnp.concatenate([got_ref[x, :ROWS, :] for x in range(NX)], axis=1)
    for z in range(0, NZ, 2):
        right = jnp.concatenate(
            [
                jnp.concatenate(
                    [got_ref[x, ROWS + (z + h) * BS : ROWS + (z + h + 1) * BS, :] for h in range(2)],
                    axis=1,
                )
                for x in range(NX)
            ],
            axis=0,
        )
        product = jnp.dot(left, right, preferred_element_type=F32).astype(BF)
        out_ref[z] = product[:, :BS]
        out_ref[z + 1] = product[:, BS:]


def sent_kernel(panel_ref, *refs):
    sent_ref = refs[-1]
    sent_ref[0, :ROWS, :] = panel_ref[...]
    for z in range(NZ):
        sent_ref[0, ROWS + z * BS : ROWS + (z + 1) * BS, :] = refs[z][...]


def weighted_kernel(at_ref, owner_ref, fill_ref, cotangent_ref, weighted_ref, meta_ref):
    for j in range(6):
        meta_ref[j] = at_ref[j]
    for j in range(NS):
        meta_ref[6 + owner_ref[j]] = j
    mine = meta_ref[6 + at_ref[3]]
    for i in range(4):
        scale = fill_ref[at_ref[4] * 4 + i, mine].astype(F32)
        rows = slice(i * BS, (i + 1) * BS)
        weighted_ref[:, rows] = (scale * cotangent_ref[rows, :]).T.astype(BF)


def tail_kernel(at_ref, fill_ref, trailing_ref, *refs):
    out_ref = refs[-1]
    mine = at_ref[6 + at_ref[3]]
    for i in range(4):
        scale = fill_ref[at_ref[4] * 4 + i, mine].astype(F32)
        rows = slice(i * BS, (i + 1) * BS)
        total = refs[0][rows, :]
        for ref in refs[1:4]:
            total += ref[rows, :].astype(F32)
        out_ref[rows, :] = trailing_ref[rows, :] - scale * total


def inner_kernel(at_ref, got_ref, factor_ref, *outs):
    right = jnp.concatenate([factor_ref[z] for z in range(NZ)], axis=1)
    rows = []
    for k in range(NX):
        x = lax.rem(at_ref[5] + k, NX)
        blocks = [got_ref[x, ROWS + z * BS : ROWS + (z + 1) * BS, :] for z in range(NZ)]
        rows.append(jnp.concatenate(blocks, axis=1))
    left = jnp.concatenate(rows, axis=0)
    product = lax.dot_general(left, right, (((1,), (1,)), ((), ())), preferred_element_type=F32)
    for k in range(NX):
        for i in range(4):
            block = product[k * BS : (k + 1) * BS, i * BS : (i + 1) * BS]
            outs[k][i] = block.astype(outs[k].dtype)


def outer_kernel(at_ref, same_ref, other_ref, factor_ref, after_ref, *outs):
    left = jnp.concatenate([factor_ref[z] for z in range(NZ)], axis=1)
    rows = []
    for k in range(NX):
        x = lax.rem(at_ref[5] + k, NX)
        mine = x // 2 == at_ref[2]
        h = lax.rem(x, 2)
        blocks = [jnp.where(mine, same_ref[z, h], other_ref[z, h]) for z in range(NZ)]
        rows.append(jnp.concatenate(blocks, axis=1))
    right = jnp.concatenate(rows, axis=0)
    product = lax.dot_general(left, right, (((1,), (1,)), ((), ())), preferred_element_type=F32)
    for k in range(NX):
        outs[k][...] = product[:, k * BS : (k + 1) * BS].astype(outs[k].dtype)


def place(at_ref, j):
    y = lax.rem(j // 8 + NY - at_ref[1], NY)
    c = lax.rem(j // 4 + at_ref[2], 2)
    return c, y, j % 4


def chosen(at_ref, j, same_ref, other_ref):
    c, y, i = place(at_ref, j)
    return jnp.where(c == 0, same_ref[y, i], other_ref[y, i])


def pick_kernel(at_ref, same_ref, other_ref, out_ref):
    for s in range(NS // 2):
        j = at_ref[6 + s // 2 * NX + s % 2 + 2 * at_ref[2]]
        out_ref[s] = chosen(at_ref, j, same_ref, other_ref)


def quarters(at_ref, refs):
    own, one, two_a, two_b, three = refs
    for k, pair in enumerate(((own, own), (one, one), (two_a, two_b), (three, three))):
        for h in range(2):
            ref = pair[h]
            first = 4 * h if ref.shape[0] == NZ else 0
            slots = []
            for d in range(4 * h, 4 * h + 4):
                z = lax.rem(at_ref[0] + d, NZ)
                x = lax.rem(at_ref[5] + k, NX)
                slots.append(at_ref[6 + z * NX + x])
            yield slots, ref[first : first + 4].reshape(4 * BS, ROWS)


def column_kernel(at_ref, *refs):
    piece_ref, same_ref, other_ref, token_ref = refs[5:]
    piece = jnp.concatenate([piece_ref[i] for i in range(4)], axis=1)
    for slots, left in quarters(at_ref, refs[:5]):
        product = lax.dot_general(
            left, piece, (((1,), (1,)), ((), ())), preferred_element_type=F32
        ).astype(BF)
        for h, j in enumerate(slots):
            c, y, i = place(at_ref, j)
            part = product[h * BS : (h + 1) * BS]
            same_ref[jnp.where(c == 0, y, NY), i] = part
            other_ref[jnp.where(c == 0, NY, y), i] = part
    token_ref[...] = jnp.zeros(token_ref.shape, F32)


def total_kernel(same_ref, got_ref, keep_ref, *outs):
    keep_ref[...] = same_ref[0].astype(F32) + got_ref[0].astype(F32)
    for k in range(1, NY):
        outs[k - 1][...] = (same_ref[k].astype(F32) + got_ref[k].astype(F32)).astype(BF)


def own_kernel(at_ref, *refs):
    all_ref, out_ref = refs[5:]
    total = jnp.zeros((BS, ROWS), F32)
    for slots, right in quarters(at_ref, refs[:5]):
        left = jnp.concatenate([all_ref[j // 4, j % 4] for j in slots], axis=1)
        total += jnp.dot(left, right, preferred_element_type=F32)
    out_ref[...] = total.T


def final_kernel(own_ref, keep_ref, *refs):
    out_ref = refs[-1]
    for i in range(4):
        rows = slice(i * BS, (i + 1) * BS)
        total = own_ref[rows, :] + keep_ref[i]
        for ref in refs[:-1]:
            total += ref[i].astype(F32)
        out_ref[rows, :] = -total


def stack_kernel(*refs):
    out_ref = refs[-1]
    for k in range(NY):
        out_ref[k] = refs[k][...]


def both_cores(pieces, *after):
    pieces = [piece.reshape(4, BS, BS) for piece in pieces]
    same = call(
        stack_kernel,
        jax.ShapeDtypeStruct((NY, 4, BS, BS), BF),
        [VMEM] * NY + [ANY] * len(after),
        0,
        1 << 20,
    )(*pieces, *after)
    return same, swap_core(same)


def whole(shape):
    return pl.BlockSpec(shape, lambda g: (0,) * len(shape))


def sweep(kernel, out_shape, *args):
    return call(
        kernel, out_shape, [SMEM] + [VMEM] * (len(args) - 1), 2 * 512 * 4096 * 128, 6 << 20
    )(*args)


def on_device(panel, inv_factor, fill, owner, trailing, cotangent):
    col = lax.axis_index("col")
    row = lax.axis_index("row")
    at = jnp.stack([col // NX, row // 2, row % 2, col, row, col % NX]).astype(jnp.int32)
    sent = pl.pallas_call(
        sent_kernel,
        grid=(NX,),
        out_shape=jax.ShapeDtypeStruct((NX, ROWS + NZ * BS, BS), BF),
        in_specs=[whole((ROWS, BS))]
        + [pl.BlockSpec((BS, BS), lambda g, z=z: (0, z * NX + g)) for z in range(NZ)],
        out_specs=pl.BlockSpec((1, ROWS + NZ * BS, BS), lambda g: (g, 0, 0)),
        cost_estimate=pl.CostEstimate(flops=0, bytes_accessed=3 << 20, transcendentals=0),
    )(panel, *([inv_factor] * NZ))
    sent, cotangent = lax.optimization_barrier((sent, cotangent))
    weighted, at = pl.pallas_call(
        weighted_kernel,
        out_shape=[
            jax.ShapeDtypeStruct((BS, ROWS), BF),
            jax.ShapeDtypeStruct((NS + 6,), jnp.int32),
        ],
        in_specs=[SMEM] * 3 + [VMEM],
        out_specs=[VMEM, SMEM],
        compiler_params=pltpu.CompilerParams(vmem_limit_bytes=16 * 1024 * 1024),
        cost_estimate=pl.CostEstimate(flops=0, bytes_accessed=1 << 19, transcendentals=0),
    )(at, owner, fill, cotangent)
    u1, d1 = shift_z(weighted, 1), shift_z(weighted, -1)
    u2, d2 = shift_z(u1, 1), shift_z(d1, -1)
    u3, d3 = shift_z(u2, 1), shift_z(d2, -1)
    half = BS // 2
    d4 = jnp.concatenate([shift_z(u3[:half], 1), shift_z(d3[half:], -1)])
    got, near = lax.optimization_barrier(
        (exchange_x(sent), jnp.stack([weighted, d1, d2, d3, d4, u3, u2, u1]))
    )

    tiles = jax.ShapeDtypeStruct((NZ, ROWS, BS), BF)
    partial = call(factor_kernel, tiles, [VMEM], 2 * 512 * 512 * 1024, 3 << 20)(got)
    parts, one, three = lax.optimization_barrier(
        (exchange_z(partial), shift_x(near, -1), shift_x(near, 1))
    )
    two_a, two_b = shift_x(three[:4], 1), shift_x(one[4:], -1)
    factor, spread = call(sum_kernel, [TILE, tiles], [VMEM], 0, 2 << 20)(parts)
    picked = call(
        pick_kernel, jax.ShapeDtypeStruct((NS // 2, BS, BS), BF), [SMEM] + [VMEM] * 2, 0, 2 << 20
    )(at, *both_cores(gather_y(factor), two_a, two_b))
    tile = jax.ShapeDtypeStruct((4, BS, BS), BF)
    total = jax.ShapeDtypeStruct((4, BS, BS), F32)
    token = jax.ShapeDtypeStruct((8, BS), F32)
    factor_k = exchange_z(spread)
    inner = call(
        inner_kernel,
        [total, tile, tile, tile],
        [SMEM] + [VMEM] * 2,
        2 * 512 * 1024 * 512,
        4 << 20,
    )(at, got, factor_k)
    owned = exchange_z(picked.reshape(NZ, 2, BS, BS))
    piece, spread = call(
        spread_kernel,
        [tile, jax.ShapeDtypeStruct((2 * NY, 4, BS, BS), BF)],
        [VMEM] * 4,
        0,
        2 << 20,
    )(inner[0], *[shift_x(inner[k], k) for k in range(1, NX)])

    weights = (near, one, two_a, two_b, three)
    blocks = jax.ShapeDtypeStruct((NY + 1, 4, BS, BS), BF)
    same, other, after = sweep(column_kernel, [blocks, blocks, token], at, *weights, piece)
    keep, *leave = call(total_kernel, [total] + [tile] * 3, [VMEM] * 2, 0, 2 << 20)(
        same, swap_core(other)
    )
    spread, after = lax.optimization_barrier((spread, after))
    own = sweep(
        own_kernel,
        jax.ShapeDtypeStruct((ROWS, BS), F32),
        at,
        *weights,
        lax.all_to_all(spread, "row", 0, 0),
    )
    moved = [shift_y(value, k + 1) for k, value in enumerate(leave)]
    panel_grad = call(
        final_kernel, jax.ShapeDtypeStruct((ROWS, BS), F32), [VMEM] * 5, 0, 1 << 20
    )(own, keep, *moved)

    outer = call(
        outer_kernel,
        [jax.ShapeDtypeStruct((ROWS, BS), F32), TILE, TILE, TILE],
        [SMEM] + [VMEM] * 3 + [ANY],
        2 * 512 * 1024 * 512,
        4 << 20,
    )(at, owned, swap_core(owned), factor_k, after)
    updated = call(
        tail_kernel, jax.ShapeDtypeStruct((ROWS, BS), F32), [SMEM] * 2 + [VMEM] * 5, 0, 1 << 20
    )(at, fill, trailing, outer[0], *[shift_x(outer[k], k) for k in range(1, NX)])
    return updated, panel_grad


def solution(mesh):
    return jax.shard_map(
        on_device,
        mesh=mesh,
        in_specs=(P("row", "col"), P("col", None), P(), P(), P("row", "col"), P("row", "col")),
        out_specs=(P("row", "col"), P("row", "col")),
        check_vma=False,
    )
```

```python
import jax
import jax.numpy as jnp
from jax import lax
from jax.experimental import pallas as pl
from jax.experimental.pallas import tpu as pltpu
from jax.sharding import PartitionSpec as P

BS = 128
NZ = 8
NX = 4
NY = 4
NS = 32
ROWS = 512
BF = jnp.bfloat16
F32 = jnp.float32
X_GROUPS = [[z * NX + x for x in range(NX)] for z in range(NZ)]
Z_GROUPS = [[z * NX + x for z in range(NZ)] for x in range(NX)]
VMEM = pl.BlockSpec(memory_space=pltpu.VMEM)
SMEM = pl.BlockSpec(memory_space=pltpu.SMEM)
ANY = pl.BlockSpec(memory_space=pl.ANY)
TILE = jax.ShapeDtypeStruct((ROWS, BS), BF)
STACK = jax.ShapeDtypeStruct((NY, ROWS, BS), BF)


def call(kernel, out_shape, in_specs, flops, nbytes, vmem=12, out_specs=None, scratch=()):
    many = isinstance(out_shape, (tuple, list))
    if out_specs is None:
        out_specs = [VMEM] * len(out_shape) if many else VMEM
    return pl.pallas_call(
        kernel,
        out_shape=out_shape,
        in_specs=in_specs,
        out_specs=out_specs,
        scratch_shapes=list(scratch),
        compiler_params=pltpu.CompilerParams(vmem_limit_bytes=vmem * 1024 * 1024),
        cost_estimate=pl.CostEstimate(flops=flops, bytes_accessed=nbytes, transcendentals=0),
    )


def exchange_x(value):
    return lax.all_to_all(value, "col", 0, 0, axis_index_groups=X_GROUPS)


def exchange_z(value):
    return lax.all_to_all(value, "col", 0, 0, axis_index_groups=Z_GROUPS)


def shift_z(value, k):
    pairs = [(z * NX + x, (z + k) % NZ * NX + x) for z in range(NZ) for x in range(NX)]
    return lax.ppermute(value, "col", pairs)


def shift_x(value, k):
    pairs = [(z * NX + x, z * NX + (x + k) % NX) for z in range(NZ) for x in range(NX)]
    return lax.ppermute(value, "col", pairs)


def shift_y(value, k):
    pairs = [(y * 2 + c, (y + k) % NY * 2 + c) for y in range(NY) for c in range(2)]
    return lax.ppermute(value, "row", pairs)


def swap_core(value):
    return lax.ppermute(value, "row", [(r, r ^ 1) for r in range(2 * NY)])


def gather_y(value):
    return [value] + [shift_y(value, -k) for k in range(1, NY)]


def spread_kernel(total_ref, *refs):
    out_ref = refs[-1]
    for i in range(4):
        total = total_ref[i]
        for ref in refs[:3]:
            total += ref[i].astype(F32)
        total = total.astype(BF)
        refs[3][i] = total
        for r in range(2 * NY):
            out_ref[r, i] = total


def sum_kernel(parts_ref, tile_ref, out_ref):
    step = 64
    for first in range(0, ROWS, step):
        rows = slice(first, first + step)
        total = parts_ref[0, rows, :].astype(F32)
        for z in range(1, NZ):
            total += parts_ref[z, rows, :].astype(F32)
        total = total.astype(BF)
        tile_ref[rows, :] = total
        for z in range(NZ):
            out_ref[z, rows, :] = total


def factor_kernel(got_ref, out_ref):
    left = jnp.concatenate([got_ref[x, :ROWS, :] for x in range(NX)], axis=1)
    for z in range(0, NZ, 2):
        right = jnp.concatenate(
            [
                jnp.concatenate(
                    [got_ref[x, ROWS + (z + h) * BS : ROWS + (z + h + 1) * BS, :] for h in range(2)],
                    axis=1,
                )
                for x in range(NX)
            ],
            axis=0,
        )
        product = jnp.dot(left, right, preferred_element_type=F32).astype(BF)
        out_ref[z] = product[:, :BS]
        out_ref[z + 1] = product[:, BS:]


def sent_kernel(panel_ref, *refs):
    sent_ref = refs[-1]
    sent_ref[0, :ROWS, :] = panel_ref[...]
    for z in range(NZ):
        sent_ref[0, ROWS + z * BS : ROWS + (z + 1) * BS, :] = refs[z][...]


def weighted_kernel(at_ref, owner_ref, fill_ref, cotangent_ref, weighted_ref, meta_ref):
    for j in range(6):
        meta_ref[j] = at_ref[j]
    for j in range(NS):
        meta_ref[6 + owner_ref[j]] = j
    mine = meta_ref[6 + at_ref[3]]
    for i in range(4):
        scale = fill_ref[at_ref[4] * 4 + i, mine].astype(F32)
        rows = slice(i * BS, (i + 1) * BS)
        weighted_ref[:, rows] = (scale * cotangent_ref[rows, :]).T.astype(BF)


def tail_kernel(at_ref, fill_ref, trailing_ref, *refs):
    out_ref = refs[-1]
    mine = at_ref[6 + at_ref[3]]
    for i in range(4):
        scale = fill_ref[at_ref[4] * 4 + i, mine].astype(F32)
        rows = slice(i * BS, (i + 1) * BS)
        total = refs[0][rows, :]
        for ref in refs[1:4]:
            total += ref[rows, :].astype(F32)
        out_ref[rows, :] = trailing_ref[rows, :] - scale * total


def inner_kernel(at_ref, got_ref, factor_ref, *outs):
    right = jnp.concatenate([factor_ref[z] for z in range(NZ)], axis=1)
    rows = []
    for k in range(NX):
        x = lax.rem(at_ref[5] + k, NX)
        blocks = [got_ref[x, ROWS + z * BS : ROWS + (z + 1) * BS, :] for z in range(NZ)]
        rows.append(jnp.concatenate(blocks, axis=1))
    left = jnp.concatenate(rows, axis=0)
    product = lax.dot_general(left, right, (((1,), (1,)), ((), ())), preferred_element_type=F32)
    for k in range(NX):
        for i in range(4):
            block = product[k * BS : (k + 1) * BS, i * BS : (i + 1) * BS]
            outs[k][i] = block.astype(outs[k].dtype)


def outer_kernel(at_ref, same_ref, other_ref, factor_ref, after_ref, *outs):
    left = jnp.concatenate([factor_ref[z] for z in range(NZ)], axis=1)
    rows = []
    for k in range(NX):
        x = lax.rem(at_ref[5] + k, NX)
        mine = x // 2 == at_ref[2]
        h = lax.rem(x, 2)
        blocks = [jnp.where(mine, same_ref[z, h], other_ref[z, h]) for z in range(NZ)]
        rows.append(jnp.concatenate(blocks, axis=1))
    right = jnp.concatenate(rows, axis=0)
    product = lax.dot_general(left, right, (((1,), (1,)), ((), ())), preferred_element_type=F32)
    for k in range(NX):
        outs[k][...] = product[:, k * BS : (k + 1) * BS].astype(outs[k].dtype)


def place(at_ref, j):
    y = lax.rem(j // 8 + NY - at_ref[1], NY)
    c = lax.rem(j // 4 + at_ref[2], 2)
    return c, y, j % 4


def chosen(at_ref, j, same_ref, other_ref):
    c, y, i = place(at_ref, j)
    return jnp.where(c == 0, same_ref[y, i], other_ref[y, i])


def pick_kernel(at_ref, same_ref, other_ref, out_ref):
    for s in range(NS // 2):
        j = at_ref[6 + s // 2 * NX + s % 2 + 2 * at_ref[2]]
        out_ref[s] = chosen(at_ref, j, same_ref, other_ref)


def quarters(at_ref, refs):
    own, one, two_a, two_b, three = refs
    for k, pair in enumerate(((own, own), (one, one), (two_a, two_b), (three, three))):
        for h in range(2):
            ref = pair[h]
            first = 4 * h if ref.shape[0] == NZ else 0
            slots = []
            for d in range(4 * h, 4 * h + 4):
                z = lax.rem(at_ref[0] + d, NZ)
                x = lax.rem(at_ref[5] + k, NX)
                slots.append(at_ref[6 + z * NX + x])
            yield slots, ref[first : first + 4].reshape(4 * BS, ROWS)


def column_kernel(at_ref, *refs):
    piece_ref, same_ref, other_ref, token_ref = refs[5:]
    piece = jnp.concatenate([piece_ref[i] for i in range(4)], axis=1)
    for slots, left in quarters(at_ref, refs[:5]):
        product = lax.dot_general(
            left, piece, (((1,), (1,)), ((), ())), preferred_element_type=F32
        ).astype(BF)
        for h, j in enumerate(slots):
            c, y, i = place(at_ref, j)
            part = product[h * BS : (h + 1) * BS]
            same_ref[jnp.where(c == 0, y, NY), i] = part
            other_ref[jnp.where(c == 0, NY, y), i] = part
    token_ref[...] = jnp.zeros(token_ref.shape, F32)


def total_kernel(same_ref, got_ref, keep_ref, *outs):
    keep_ref[...] = same_ref[0].astype(F32) + got_ref[0].astype(F32)
    for k in range(1, NY):
        outs[k - 1][...] = (same_ref[k].astype(F32) + got_ref[k].astype(F32)).astype(BF)


def own_kernel(at_ref, *refs):
    all_ref, out_ref = refs[5:]
    total = jnp.zeros((BS, ROWS), F32)
    for slots, right in quarters(at_ref, refs[:5]):
        left = jnp.concatenate([all_ref[j // 4, j % 4] for j in slots], axis=1)
        total += jnp.dot(left, right, preferred_element_type=F32)
    out_ref[...] = total.T


def final_kernel(own_ref, keep_ref, *refs):
    out_ref = refs[-1]
    for i in range(4):
        rows = slice(i * BS, (i + 1) * BS)
        total = own_ref[rows, :] + keep_ref[i]
        for ref in refs[:-1]:
            total += ref[i].astype(F32)
        out_ref[rows, :] = -total


def stack_kernel(*refs):
    out_ref = refs[-1]
    for k in range(NY):
        out_ref[k] = refs[k][...]


def both_cores(pieces, *after):
    pieces = [piece.reshape(4, BS, BS) for piece in pieces]
    same = call(
        stack_kernel,
        jax.ShapeDtypeStruct((NY, 4, BS, BS), BF),
        [VMEM] * NY + [ANY] * len(after),
        0,
        1 << 20,
    )(*pieces, *after)
    return same, swap_core(same)


def whole(shape):
    return pl.BlockSpec(shape, lambda g: (0,) * len(shape))


def sweep(kernel, out_shape, *args):
    return call(
        kernel, out_shape, [SMEM] + [VMEM] * (len(args) - 1), 2 * 512 * 4096 * 128, 6 << 20
    )(*args)


def on_device(panel, inv_factor, fill, owner, trailing, cotangent):
    col = lax.axis_index("col")
    row = lax.axis_index("row")
    at = jnp.stack([col // NX, row // 2, row % 2, col, row, col % NX]).astype(jnp.int32)
    sent = pl.pallas_call(
        sent_kernel,
        grid=(NX,),
        out_shape=jax.ShapeDtypeStruct((NX, ROWS + NZ * BS, BS), BF),
        in_specs=[whole((ROWS, BS))]
        + [pl.BlockSpec((BS, BS), lambda g, z=z: (0, z * NX + g)) for z in range(NZ)],
        out_specs=pl.BlockSpec((1, ROWS + NZ * BS, BS), lambda g: (g, 0, 0)),
        cost_estimate=pl.CostEstimate(flops=0, bytes_accessed=3 << 20, transcendentals=0),
    )(panel, *([inv_factor] * NZ))
    sent, cotangent = lax.optimization_barrier((sent, cotangent))
    weighted, at = pl.pallas_call(
        weighted_kernel,
        out_shape=[
            jax.ShapeDtypeStruct((BS, ROWS), BF),
            jax.ShapeDtypeStruct((NS + 6,), jnp.int32),
        ],
        in_specs=[SMEM] * 3 + [VMEM],
        out_specs=[VMEM, SMEM],
        compiler_params=pltpu.CompilerParams(vmem_limit_bytes=16 * 1024 * 1024),
        cost_estimate=pl.CostEstimate(flops=0, bytes_accessed=1 << 19, transcendentals=0),
    )(at, owner, fill, cotangent)
    u1, d1 = shift_z(weighted, 1), shift_z(weighted, -1)
    u2, d2 = shift_z(u1, 1), shift_z(d1, -1)
    u3, d3 = shift_z(u2, 1), shift_z(d2, -1)
    half = BS // 2
    d4 = jnp.concatenate([shift_z(u3[:half], 1), shift_z(d3[half:], -1)])
    got, near = lax.optimization_barrier(
        (exchange_x(sent), jnp.stack([weighted, d1, d2, d3, d4, u3, u2, u1]))
    )

    tiles = jax.ShapeDtypeStruct((NZ, ROWS, BS), BF)
    partial = call(factor_kernel, tiles, [VMEM], 2 * 512 * 512 * 1024, 3 << 20)(got)
    parts, one, three = lax.optimization_barrier(
        (exchange_z(partial), shift_x(near, -1), shift_x(near, 1))
    )
    two_a, two_b = shift_x(three[:4], 1), shift_x(one[4:], -1)
    factor, spread = call(sum_kernel, [TILE, tiles], [VMEM], 0, 2 << 20)(parts)
    picked = call(
        pick_kernel, jax.ShapeDtypeStruct((NS // 2, BS, BS), BF), [SMEM] + [VMEM] * 2, 0, 2 << 20
    )(at, *both_cores(gather_y(factor), two_a, two_b))
    tile = jax.ShapeDtypeStruct((4, BS, BS), BF)
    total = jax.ShapeDtypeStruct((4, BS, BS), F32)
    token = jax.ShapeDtypeStruct((8, BS), F32)
    factor_k = exchange_z(spread)
    inner = call(
        inner_kernel,
        [total, tile, tile, tile],
        [SMEM] + [VMEM] * 2,
        2 * 512 * 1024 * 512,
        4 << 20,
    )(at, got, factor_k)
    owned = exchange_z(picked.reshape(NZ, 2, BS, BS))
    piece, spread = call(
        spread_kernel,
        [tile, jax.ShapeDtypeStruct((2 * NY, 4, BS, BS), BF)],
        [VMEM] * 4,
        0,
        2 << 20,
    )(inner[0], *[shift_x(inner[k], k) for k in range(1, NX)])

    weights = (near, one, two_a, two_b, three)
    blocks = jax.ShapeDtypeStruct((NY + 1, 4, BS, BS), BF)
    same, other, after = sweep(column_kernel, [blocks, blocks, token], at, *weights, piece)
    keep, *leave = call(total_kernel, [total] + [tile] * 3, [VMEM] * 2, 0, 2 << 20)(
        same, swap_core(other)
    )
    spread, after = lax.optimization_barrier((spread, after))
    own = sweep(
        own_kernel,
        jax.ShapeDtypeStruct((ROWS, BS), F32),
        at,
        *weights,
        lax.all_to_all(spread, "row", 0, 0),
    )
    moved = [shift_y(value, k + 1) for k, value in enumerate(leave)]
    panel_grad = call(
        final_kernel, jax.ShapeDtypeStruct((ROWS, BS), F32), [VMEM] * 5, 0, 1 << 20
    )(own, keep, *moved)

    outer = call(
        outer_kernel,
        [jax.ShapeDtypeStruct((ROWS, BS), F32), TILE, TILE, TILE],
        [SMEM] + [VMEM] * 3 + [ANY],
        2 * 512 * 1024 * 512,
        4 << 20,
    )(at, owned, swap_core(owned), factor_k, after)
    updated = call(
        tail_kernel, jax.ShapeDtypeStruct((ROWS, BS), F32), [SMEM] * 2 + [VMEM] * 5, 0, 1 << 20
    )(at, fill, trailing, outer[0], *[shift_x(outer[k], k) for k in range(1, NX)])
    return updated, panel_grad


def solution(mesh):
    return jax.shard_map(
        on_device,
        mesh=mesh,
        in_specs=(P("row", "col"), P("col", None), P(), P(), P("row", "col"), P("row", "col")),
        out_specs=(P("row", "col"), P("row", "col")),
        check_vma=False,
    )
```
